256 devices in a mesh: space: 32 (over z, x), tm: 8 (over y, core).
Axes of the slice: x: 4, y: 4, z: 8, core: 2. Of those that a mesh axis runs over, the one named last changes fastest.
Arguments:
- frame_slab: float32 [65536, 4096], P('space', 'tm'), may hold values from -160 to 160
- pair_decay_rates: float32 [32], replicated, may hold values from -2 to 0.5
- pair_angular_frequencies: float32 [32], replicated, as said below
Outputs:
- spatial_modes: float32 [64, 65536], P(None, 'space')
- misfit_matrix: float32 [65536, 4096], P('space', 'tm')
- gradient: float32 [64], replicated
- gauss_newton: float32 [64, 64], replicated
The draws below stay inside these ranges and needn't reach their ends.
Inputs may be any that keep to these rules, and one draw needn't show every extreme that they name: pair_angular_frequencies[k] lies within 0.5 of 2 pi (k + 1).
All inputs are finite; a program needn't handle non-finite values.
Results may differ from the reference program's by a relative error of at most 0.0003.
Values sent between devices are 32-bit elements; how exact they have to be, the bound alone decides.
No kernel may reach another device: no remote copies, remote signals or barrier semaphores. Data moves between devices by JAX's collectives and lax.ppermute only.
A program may use at most 64 MiB of HBM per device.

```python
import jax
import jax.numpy as jnp
from jax import lax

PAIRS = 32
NP = 65536
FRAME_NUMBER = 4096
N_SPACE = 32


def draw_frame_slab(key, part):
    key = jax.random.fold_in(key, 11)
    streams = jax.random.split(key, 7)
    positions = jnp.arange(NP, dtype=jnp.float32) / NP
    measured_epochs = jnp.arange(FRAME_NUMBER, dtype=jnp.float32) / FRAME_NUMBER
    multiplier_power = jax.random.uniform(streams[0], (4,), minval=-1.5, maxval=0.3)
    cycle_spacings = jax.random.uniform(streams[1], (4,), minval=5.0, maxval=150.0)
    amplitudes = jax.random.uniform(streams[2], (NP, 4), minval=-1.0, maxval=1.0)
    argument_radians = jax.random.uniform(streams[3], (NP, 4), minval=-jnp.pi, maxval=jnp.pi)
    signal = jnp.zeros((NP, FRAME_NUMBER), jnp.float32)
    for mode_profile_entry in range(4):
        cycle_cosine_term = jnp.exp(multiplier_power[mode_profile_entry] * measured_epochs)[None, :] * jnp.cos(cycle_spacings[mode_profile_entry] * measured_epochs[None, :] + argument_radians[:, mode_profile_entry:mode_profile_entry + 1])
        signal = signal + amplitudes[:, mode_profile_entry:mode_profile_entry + 1] * cycle_cosine_term
    noise_part = jax.random.truncated_normal(streams[4], -4.0, 4.0, (NP, FRAME_NUMBER))
    spread = jnp.log(10.0)
    levels = jax.random.uniform(streams[5], (NP,), minval=0.0, maxval=1.0)
    row_scale = jnp.exp(jnp.log(3.0) * positions + levels * (spread - jnp.log(3.0)))
    noise_level = jnp.exp(jax.random.uniform(streams[6], (1, FRAME_NUMBER), minval=jnp.log(0.3), maxval=jnp.log(0.9)))
    return (row_scale[:, None] * (signal + noise_level * noise_part)).astype(jnp.float32)


def draw_pair_angular_frequencies(key, part):
    key = jax.random.fold_in(key, 5)
    offsets = jax.random.uniform(key, (PAIRS,), minval=-0.5, maxval=0.5)
    return (2.0 * jnp.pi * (jnp.arange(PAIRS, dtype=jnp.float32) + 1.0) + offsets).astype(jnp.float32)


def setup_inputs(seed: int = 0) -> dict:
    key_list = jax.random.split(jax.random.key(seed), 4)
    frame_slab = draw_frame_slab(jax.random.fold_in(key_list[3], 71), 0)
    pair_decay_rates = jnp.clip(jax.random.uniform(key_list[1], (PAIRS,), jnp.float32, -2.0, 0.5), -2.0, 0.5)
    pair_angular_frequencies = draw_pair_angular_frequencies(jax.random.fold_in(key_list[3], 71), 0)
    return dict(frame_slab=frame_slab, pair_decay_rates=pair_decay_rates, pair_angular_frequencies=pair_angular_frequencies)


highest = lax.Precision.HIGHEST

def build_epoch_vectors(pair_decay_rates, pair_angular_frequencies, measured_epochs):
    shrinking_exponential = jnp.exp(pair_decay_rates[:, None] * measured_epochs[None, :])
    turning_radians = pair_angular_frequencies[:, None] * measured_epochs[None, :]
    joined_vectors = jnp.stack([shrinking_exponential * jnp.cos(turning_radians), shrinking_exponential * jnp.sin(turning_radians)], axis=1)
    return joined_vectors.reshape(2 * pair_decay_rates.shape[0], measured_epochs.shape[0])

def coupling_table():
    return jnp.array([[[1.0, 0.0], [0.0, 1.0]], [[0.0, -1.0], [1.0, 0.0]]], dtype=jnp.float32)

def newton_terms(cross_term, mode_gram, slope_gram, magnitude_divisor):
    pairs = cross_term.shape[0] // 2
    coupling = coupling_table()
    cross_blocks = cross_term.reshape(pairs, 2, pairs, 2)
    indices = jnp.arange(pairs, dtype=jnp.int32)
    diagonal_blocks = cross_blocks[indices, :, indices, :]
    gradient = -magnitude_divisor * jnp.einsum('puw,kuw->kp', coupling, diagonal_blocks, precision=highest)
    mode_blocks = mode_gram.reshape(pairs, 2, pairs, 2)
    slope_blocks = slope_gram.reshape(pairs, 2, pairs, 2)
    inner = jnp.einsum('kulv,kwlx->kuwlvx', mode_blocks, slope_blocks, precision=highest)
    gauss_newton = magnitude_divisor * jnp.einsum('puw,kuwlvx,qvx->kplq', coupling, inner, coupling, precision=highest)
    return (gradient.reshape(2 * pairs), gauss_newton.reshape(2 * pairs, 2 * pairs))

def reference(frame_slab, pair_decay_rates, pair_angular_frequencies):
    location_number, complete_epochs = frame_slab.shape
    measured_epochs = jnp.arange(complete_epochs, dtype=jnp.float32) / complete_epochs
    epoch_vector_set = build_epoch_vectors(pair_decay_rates, pair_angular_frequencies, measured_epochs)
    jacobian_lines = epoch_vector_set * measured_epochs[None, :]
    basis_gram = jnp.dot(epoch_vector_set.astype(jnp.float32), epoch_vector_set.T.astype(jnp.float32), precision=highest, preferred_element_type=jnp.float32)
    slope_gram = jnp.dot(jacobian_lines.astype(jnp.float32), jacobian_lines.T.astype(jnp.float32), precision=highest, preferred_element_type=jnp.float32)
    projection = lax.dot_general(epoch_vector_set.astype(jnp.float32), frame_slab.astype(jnp.float32), (((1,), (1,)), ((), ())), precision=highest, preferred_element_type=jnp.float32)
    factor = jnp.linalg.cholesky(basis_gram)
    spatial_modes = jax.scipy.linalg.cho_solve((factor, True), projection)
    segment_locations = location_number // N_SPACE
    segment_list = frame_slab.reshape(N_SPACE, segment_locations, complete_epochs)
    mode_blocks = spatial_modes.reshape(-1, N_SPACE, segment_locations).transpose(1, 0, 2)

    def block_terms(block_pair):
        block_rows, block_modes = block_pair
        fitted = lax.dot_general(block_modes.astype(jnp.float32), epoch_vector_set.astype(jnp.float32), (((0,), (0,)), ((), ())), precision=highest, preferred_element_type=jnp.float32)
        block_residual = block_rows - fitted
        moment = lax.dot_general(block_residual.astype(jnp.float32), jacobian_lines.astype(jnp.float32), (((1,), (1,)), ((), ())), precision=highest, preferred_element_type=jnp.float32)
        return (block_residual, jnp.dot(block_modes.astype(jnp.float32), moment.astype(jnp.float32), precision=highest, preferred_element_type=jnp.float32))
    misfit_segments, cross_parts = lax.map(block_terms, (segment_list, mode_blocks))
    misfit_matrix = misfit_segments.reshape(location_number, complete_epochs)
    cross_term = jnp.sum(cross_parts, axis=0)
    mode_gram = jnp.dot(spatial_modes.astype(jnp.float32), spatial_modes.T.astype(jnp.float32), precision=highest, preferred_element_type=jnp.float32)
    magnitude_divisor = 1.0 / (location_number * complete_epochs)
    gradient, gauss_newton = newton_terms(cross_term, mode_gram, slope_gram, magnitude_divisor)
    return (spatial_modes, misfit_matrix, gradient, gauss_newton)
```

```python
import jax
import jax.numpy as jnp
from jax import lax
from jax.experimental import pallas as pl
from jax.experimental.pallas import tpu as pltpu
from jax.sharding import PartitionSpec as P

f32 = jnp.float32
bf16 = jnp.bfloat16
highest = lax.Precision.HIGHEST
VMEM = pl.BlockSpec(memory_space=pltpu.VMEM)
ANY = pl.BlockSpec(memory_space=pl.ANY)
PARAMS = pltpu.CompilerParams(vmem_limit_bytes=40 * 1024 * 1024)


def dot(a, b, precision=None):
    return lax.dot_general(
        a, b, (((1,), (0,)), ((), ())), precision=precision, preferred_element_type=f32
    )


def dot_nt(a, b, precision=None):
    return lax.dot_general(
        a, b, (((1,), (1,)), ((), ())), precision=precision, preferred_element_type=f32
    )


def split(x):
    hi = x.astype(bf16)
    lo = (x - hi.astype(f32)).astype(bf16)
    return hi, lo


def sine_or_cosine(theta, is_cosine):
    q = jnp.floor(theta * 0.6366197723675814 + 0.5)
    r = theta - q * 1.5703125
    r = r - q * 4.837512969970703125e-4
    r = r - q * 7.5497899548918821691e-8
    s = r * r
    sine = r + r * s * (
        -0.16666666666 + s * (0.0083333293858894631756 + s * (-0.000198393348360966317347 + s * 2.7181216275479732e-6))
    )
    cosine = 1.0 + s * (
        -0.5 + s * (0.0416666641831398010253906 + s * (-0.001388833043165504932 + s * 2.4390448796277409e-5))
    )
    n = q.astype(jnp.int32) + jnp.where(is_cosine, 1, 0)
    value = jnp.where((n & 1) == 1, cosine, sine)
    return jnp.where((n & 2) == 2, -value, value)


def lane_parameters(values):
    n = values.shape[1]
    rows = lax.broadcasted_iota(jnp.int32, (n, 4 * n), 0)
    lanes = lax.broadcasted_iota(jnp.int32, (n, 4 * n), 1)
    eye = lax.broadcasted_iota(jnp.int32, (n, n), 0) == lax.broadcasted_iota(jnp.int32, (n, n), 1)
    column = jnp.sum(jnp.where(eye, values, 0.0), axis=1, keepdims=True)
    hit = (lanes % (2 * n)) // 2 == rows
    return jnp.sum(jnp.where(hit, column, 0.0), axis=0, keepdims=True)


def basis_and_slope(rates, freqs, first, count, complete):
    width = 4 * rates.shape[1]
    rate = lane_parameters(rates)
    freq = lane_parameters(freqs)
    lanes = lax.broadcasted_iota(jnp.int32, (count, width), 1)
    steps = lax.broadcasted_iota(jnp.int32, (count, width), 0) + first
    t = steps.astype(f32) / complete
    value = jnp.exp(rate * t) * sine_or_cosine(freq * t, lanes % 2 == 0)
    return jnp.where(lanes < width // 2, value, value * t)


def half_index(tm):
    return (tm + tm // 2) % 2


def load_half(d_ref, buf, sems, start, chunks):
    rows = buf.shape[0] // chunks
    copies = []
    for i in range(chunks):
        piece = pl.ds(i * rows, rows)
        copy = pltpu.make_async_copy(
            d_ref.at[pl.ds(pl.multiple_of(start + i * rows, rows), rows)], buf.at[piece], sems.at[i]
        )
        copy.start()
        copies.append(copy)
    return copies


def project(copies, buf, w, out_ref):
    chunks = len(copies)
    rows = buf.shape[0] // chunks
    width = out_ref.shape[1]
    for i, copy in enumerate(copies):
        copy.wait()
        piece = pl.ds(i * rows, rows)
        hi, lo = split(buf[piece, :])
        both = dot(hi, w) + dot(lo, w)
        out_ref[piece, :] = both[:, :width] + both[:, width:]


def first_kernel(complete, d_ref, rates_ref, freqs_ref, out_ref, w_ref, buf, sems):
    tm = lax.axis_index("tm")
    half = buf.shape[0]
    copies = load_half(d_ref, buf, sems, (1 - half_index(tm)) * half, sems.shape[0])
    count = d_ref.shape[1]
    x = basis_and_slope(rates_ref[...], freqs_ref[...], tm * count, count, complete)
    hi, lo = split(x)
    width = x.shape[1]
    w_ref[:, :width] = hi
    w_ref[:, width:] = lo
    project(copies, buf, w_ref[...], out_ref)


def second_kernel(d_ref, w_ref, out_ref, buf, sems):
    tm = lax.axis_index("tm")
    half = buf.shape[0]
    copies = load_half(d_ref, buf, sems, half_index(tm) * half, sems.shape[0])
    project(copies, buf, w_ref[...], out_ref)


def swap_rows(x):
    rows = lax.broadcasted_iota(jnp.int32, x.shape, 0)
    n = x.shape[0]
    return jnp.where(rows % 2 == 0, pltpu.roll(x, n - 1, 0), pltpu.roll(x, 1, 0))


def swap_lanes(x):
    lanes = lax.broadcasted_iota(jnp.int32, x.shape, 1)
    n = x.shape[1]
    return jnp.where(lanes % 2 == 0, pltpu.roll(x, n - 1, 1), pltpu.roll(x, 1, 1))


def inverse(a):
    n = a.shape[0]
    rows = lax.broadcasted_iota(jnp.int32, (n, n), 0)
    lanes = lax.broadcasted_iota(jnp.int32, (n, n), 1)
    for j in range(n):
        pivot_row = a[j : j + 1, :]
        column = a[:, j : j + 1]
        scale = 1.0 / a[j : j + 1, j : j + 1]
        scaled = jnp.where(lanes[:1] == j, scale, pivot_row * scale)
        rest = jnp.where(lanes == j, 0.0, a) - column * scaled
        a = jnp.where(rows == j, scaled, rest)
    return a


def gram_kernel(complete, rates_ref, freqs_ref, after_ref, inverse_ref, slope_ref, basis_slope_ref, x_ref):
    del after_ref
    width = 4 * rates_ref.shape[1]
    half = width // 2
    x_ref[...] = basis_and_slope(rates_ref[...], freqs_ref[...], 0, complete, complete)
    total = jnp.zeros((width, width), f32)
    block = 1024
    for i in range(complete // block):
        x = x_ref[pl.ds(i * block, block), :]
        total = total + lax.dot_general(
            x, x, (((0,), (0,)), ((), ())), precision=highest, preferred_element_type=f32
        )
    gram = total[:half, :half]
    inv = inverse(gram)
    inverse_ref[...] = jnp.concatenate(
        [jnp.concatenate([inv, jnp.zeros_like(inv)], axis=1), jnp.zeros((half, width), f32)], axis=0
    )
    slope = pltpu.roll(total[half:, :], half, 1)
    lanes = lax.broadcasted_iota(jnp.int32, slope.shape, 1)
    rows = lax.broadcasted_iota(jnp.int32, slope.shape, 0)
    row_sign = jnp.where(rows % 2 == 0, -1.0, 1.0)
    lane_sign = jnp.where(lanes % 2 == 0, -1.0, 1.0)
    turned = row_sign * swap_rows(slope)
    slope_ref[0] = slope
    slope_ref[1] = lane_sign * swap_lanes(slope)
    slope_ref[2] = turned
    slope_ref[3] = lane_sign * swap_lanes(turned)
    basis_slope_ref[...] = pltpu.roll(total[:half, :], half, 1)


def modes_kernel(a_ref, b_ref, inverse_ref, modes_ref, message_ref):
    x = a_ref[...] + b_ref[...]
    width = x.shape[1]
    half = width // 2
    lanes = lax.broadcasted_iota(jnp.int32, x.shape, 1)
    x = jnp.where(lanes < half, dot(x, inverse_ref[...], highest), x)
    modes = jnp.transpose(x)[:half]
    modes_ref[...] = modes
    both = dot(modes, x, highest)
    rows = lax.broadcasted_iota(jnp.int32, both.shape, 0)
    lanes = lax.broadcasted_iota(jnp.int32, both.shape, 1)
    low = both[: half // 2]
    high = pltpu.roll(both[half // 2 :], half, 1)
    message_ref[: half // 2] = jnp.where(lanes[: half // 2] < half, low, high)
    column = lanes - half
    same = jnp.sum(jnp.where(rows == column, both, 0.0), axis=0, keepdims=True)
    swapped = jnp.where(column % 2 == 0, both, -both)
    partner = jnp.where(column % 2 == 0, column + 1, column - 1)
    turn = jnp.sum(jnp.where(rows == partner, swapped, 0.0), axis=0, keepdims=True)
    tail = lax.broadcasted_iota(jnp.int32, (8, width), 0)
    message_ref[half // 2 :] = jnp.where(tail == 0, same, jnp.where(tail == 1, turn, 0.0))


def misfit_kernel(d_ref, own_ref, other_ref, w_ref, modes_ref, misfit_ref, b_ref):
    tm = lax.axis_index("tm")
    step = pl.program_id(0)
    steps = pl.num_programs(0)
    half, width = own_ref.shape[0], 2 * own_ref.shape[0]

    @pl.when(step == 0)
    def _():
        top = jnp.transpose(w_ref[:, :width].astype(f32))[:half].astype(bf16)
        low = jnp.transpose(w_ref[:, width:].astype(f32))[:half].astype(bf16)
        b_ref[...] = jnp.concatenate([top, low, top, low], axis=0)

    rows = d_ref.shape[0]
    mine = (step // (steps // 2)) == half_index(tm)
    place = pl.ds(pl.multiple_of((step % (steps // 2)) * rows, rows), rows)
    modes = jnp.where(mine, own_ref[:, place], other_ref[:, place])
    modes_ref[...] = modes
    hi, lo = split(jnp.transpose(jnp.concatenate([modes, modes], axis=0)))
    fitted = dot(jnp.concatenate([hi, lo], axis=1), b_ref[...])
    misfit_ref[...] = d_ref[...] - fitted


def last_kernel(divisor, a_ref, b_ref, slope_ref, basis_slope_ref, gradient_ref, newton_ref):
    m = a_ref[...] + b_ref[...]
    width = m.shape[1]
    half = width // 2
    quarter = half // 2
    upper = m[:quarter]
    gram = jnp.concatenate([upper, pltpu.roll(upper, half, 1)], axis=0)
    rows = lax.broadcasted_iota(jnp.int32, gram.shape, 0)
    lanes = lax.broadcasted_iota(jnp.int32, gram.shape, 1)

    def block_sums(x):
        y = x + swap_rows(x)
        return y + swap_lanes(y)

    def for_row(first, second):
        return jnp.where(rows % 2 == 0, first, second)

    even = for_row(block_sums(gram * slope_ref[0]), block_sums(gram * slope_ref[2]))
    odd = for_row(block_sums(gram * slope_ref[1]), block_sums(gram * slope_ref[3]))
    newton = divisor * jnp.where(lanes % 2 == 0, even, odd)
    newton_ref[...] = newton[:, :half]
    basis_slope = basis_slope_ref[...]
    same = jnp.sum(gram * basis_slope, axis=0, keepdims=True)
    turn = jnp.sum(swap_lanes(gram) * basis_slope, axis=0, keepdims=True)
    tail = pltpu.roll(m[quarter:], half, 1)
    lane = lanes[:1]
    same = tail[0:1] - same
    turn = tail[1:2] - jnp.where(lane % 2 == 0, turn, -turn)
    same = same + swap_lanes(same)
    turn = turn + swap_lanes(turn)
    gradient_ref[...] = (-divisor * jnp.where(lane % 2 == 0, same, turn))[:, :half]


def flips(n, bits):
    return [(i, i ^ bits) for i in range(n)]


def local(frame_slab, pair_decay_rates, pair_angular_frequencies):
    points, epochs = frame_slab.shape
    pairs = pair_decay_rates.shape[0]
    basis = 2 * pairs
    width = 2 * basis
    tm_size, space_size = lax.axis_size("tm"), lax.axis_size("space")
    complete = epochs * tm_size
    half = points // 2
    divisor = 1.0 / (points * space_size * complete)
    rates = pair_decay_rates.reshape(1, pairs)
    freqs = pair_angular_frequencies.reshape(1, pairs)
    chunks = 4
    scratch = [pltpu.VMEM((half, epochs), f32), pltpu.SemaphoreType.DMA((chunks,))]

    away, w = pl.pallas_call(
        lambda *refs: first_kernel(complete, *refs),
        out_shape=(
            jax.ShapeDtypeStruct((half, width), f32),
            jax.ShapeDtypeStruct((epochs, 2 * width), bf16),
        ),
        in_specs=[ANY, VMEM, VMEM],
        out_specs=(VMEM, VMEM),
        scratch_shapes=scratch,
        compiler_params=PARAMS,
        name="project_away",
    )(frame_slab, rates, freqs)
    arrived = lax.ppermute(away, "tm", flips(tm_size, 1))
    kept = pl.pallas_call(
        second_kernel,
        out_shape=jax.ShapeDtypeStruct((half, width), f32),
        in_specs=[ANY, VMEM],
        out_specs=VMEM,
        scratch_shapes=scratch,
        compiler_params=PARAMS,
        cost_estimate=pl.CostEstimate(flops=2 * half * epochs * width * 4, bytes_accessed=half * epochs * 4, transcendentals=0),
        name="project_kept",
    )(frame_slab, w)
    inverse_gram, slopes, basis_slope = pl.pallas_call(
        lambda *refs: gram_kernel(complete, *refs),
        out_shape=(
            jax.ShapeDtypeStruct((width, width), f32),
            jax.ShapeDtypeStruct((4, basis, width), f32),
            jax.ShapeDtypeStruct((basis, width), f32),
        ),
        in_specs=[VMEM, VMEM, ANY],
        out_specs=(VMEM, VMEM, VMEM),
        scratch_shapes=[pltpu.VMEM((complete, width), f32)],
        compiler_params=PARAMS,
        cost_estimate=pl.CostEstimate(flops=10**9, bytes_accessed=10**7, transcendentals=10**6),
        name="grams",
    )(rates, freqs, kept)

    summed = kept + arrived
    quarter = half // 2
    first, second = summed[:quarter], summed[quarter:]
    near, wrap = flips(tm_size, 3), flips(tm_size, 7)
    first_in = lax.ppermute(first, "tm", near)
    second_in = lax.ppermute(second, "tm", wrap)
    first = first + first_in
    second = second + second_in
    first_in = lax.ppermute(first, "tm", wrap)
    second_in = lax.ppermute(second, "tm", near)
    modes_half, message = pl.pallas_call(
        modes_kernel,
        out_shape=(
            jax.ShapeDtypeStruct((basis, half), f32),
            jax.ShapeDtypeStruct((pairs + 8, width), f32),
        ),
        in_specs=[VMEM] * 3,
        out_specs=(VMEM, VMEM),
        compiler_params=PARAMS,
        name="modes",
    )(jnp.concatenate([first, second]), jnp.concatenate([first_in, second_in]), inverse_gram)

    message = message + lax.ppermute(message, "tm", flips(tm_size, 1))
    modes_other = lax.ppermute(modes_half, "tm", flips(tm_size, 1))
    block = 256
    steps = points // block
    spatial_modes, misfit = pl.pallas_call(
        misfit_kernel,
        grid=(steps,),
        out_shape=(
            jax.ShapeDtypeStruct((basis, points), f32),
            jax.ShapeDtypeStruct((points, epochs), f32),
        ),
        in_specs=[pl.BlockSpec((block, epochs), lambda i: (i, 0)), VMEM, VMEM, VMEM],
        out_specs=(
            pl.BlockSpec((basis, block), lambda i: (0, i)),
            pl.BlockSpec((block, epochs), lambda i: (i, 0)),
        ),
        scratch_shapes=[pltpu.VMEM((width * 2, epochs), bf16)],
        compiler_params=PARAMS,
        cost_estimate=pl.CostEstimate(flops=10**9, bytes_accessed=10**7, transcendentals=0),
        name="misfit",
    )(frame_slab, modes_half, modes_other, w)
    axes = ("space", "tm")
    total = space_size * tm_size
    incoming = None
    for bits in (1, 3, 4, 12, 28):
        if incoming is not None:
            message = message + incoming
        incoming = lax.ppermute(message, axes, flips(total, bits * tm_size + 1))
    gradient, gauss_newton = pl.pallas_call(
        lambda *refs: last_kernel(divisor, *refs),
        out_shape=(
            jax.ShapeDtypeStruct((1, basis), f32),
            jax.ShapeDtypeStruct((basis, basis), f32),
        ),
        in_specs=[VMEM] * 4,
        out_specs=(VMEM, VMEM),
        compiler_params=PARAMS,
        name="newton",
    )(message, incoming, slopes, basis_slope)
    return spatial_modes, misfit, gradient.reshape(basis), gauss_newton


def solution(mesh):
    return jax.shard_map(
        local,
        mesh=mesh,
        in_specs=(P("space", "tm"), P(), P()),
        out_specs=(P(None, "space"), P("space", "tm"), P(), P()),
        check_vma=False,
    )
```

```python
import jax
import jax.numpy as jnp
from jax import lax
from jax.experimental import pallas as pl
from jax.experimental.pallas import tpu as pltpu
from jax.sharding import PartitionSpec as P

f32 = jnp.float32
bf16 = jnp.bfloat16
highest = lax.Precision.HIGHEST
VMEM = pl.BlockSpec(memory_space=pltpu.VMEM)
HBM = pl.BlockSpec(memory_space=pltpu.HBM)
ANY = pl.BlockSpec(memory_space=pl.ANY)
PARAMS = pltpu.CompilerParams(vmem_limit_bytes=40 * 1024 * 1024)


def dot(a, b, precision=None):
    return lax.dot_general(
        a, b, (((1,), (0,)), ((), ())), precision=precision, preferred_element_type=f32
    )


def dot_nt(a, b, precision=None):
    return lax.dot_general(
        a, b, (((1,), (1,)), ((), ())), precision=precision, preferred_element_type=f32
    )


def split(x):
    hi = x.astype(bf16)
    lo = (x - hi.astype(f32)).astype(bf16)
    return hi, lo


def sine_or_cosine(theta, is_cosine):
    q = jnp.floor(theta * 0.6366197723675814 + 0.5)
    r = theta - q * 1.5703125
    r = r - q * 4.837512969970703125e-4
    r = r - q * 7.5497899548918821691e-8
    s = r * r
    sine = r + r * s * (
        -0.16666666666 + s * (0.0083333293858894631756 + s * (-0.000198393348360966317347 + s * 2.7181216275479732e-6))
    )
    cosine = 1.0 + s * (
        -0.5 + s * (0.0416666641831398010253906 + s * (-0.001388833043165504932 + s * 2.4390448796277409e-5))
    )
    n = q.astype(jnp.int32) + jnp.where(is_cosine, 1, 0)
    value = jnp.where((n & 1) == 1, cosine, sine)
    return jnp.where((n & 2) == 2, -value, value)


def lane_parameters(values):
    n = values.shape[1]
    rows = lax.broadcasted_iota(jnp.int32, (n, 4 * n), 0)
    lanes = lax.broadcasted_iota(jnp.int32, (n, 4 * n), 1)
    eye = lax.broadcasted_iota(jnp.int32, (n, n), 0) == lax.broadcasted_iota(jnp.int32, (n, n), 1)
    column = jnp.sum(jnp.where(eye, values, 0.0), axis=1, keepdims=True)
    hit = (lanes % (2 * n)) // 2 == rows
    return jnp.sum(jnp.where(hit, column, 0.0), axis=0, keepdims=True)


def decayed_waves(rates, freqs, t):
    lanes = lax.broadcasted_iota(jnp.int32, t.shape, 1)
    rate = lane_parameters(rates)
    freq = lane_parameters(freqs)
    return jnp.exp(rate * t) * sine_or_cosine(freq * t, lanes % 2 == 0)


def half_index(tm):
    return (tm + tm // 2) % 2


def load_half(d_hbm, buf, sems, side):
    half = buf.shape[0]
    rows = half // sems.shape[0]
    copies = []
    for i in range(sems.shape[0]):
        piece = pl.ds(pl.multiple_of(side * half + i * rows, rows), rows)
        copies.append(pltpu.make_async_copy(d_hbm.at[piece], buf.at[pl.ds(i * rows, rows)], sems.at[i]))
        copies[-1].start()
    return copies


def project(copies, buf, w, out_ref):
    width = out_ref.shape[1]
    half = width // 2
    count = out_ref.shape[0] // 2
    for copy in copies:
        copy.wait()

    def product(start):
        hi, lo = split(buf[start : start + count, :])
        both = dot(hi, w) + dot(lo, w)
        return both[:, :width] + both[:, width:]

    x, y = product(0), product(count)
    left = lax.broadcasted_iota(jnp.int32, x.shape, 1) < half
    out_ref[:count, :] = jnp.where(left, x, pltpu.roll(y, half, 1))
    out_ref[count:, :] = jnp.where(left, pltpu.roll(x, half, 1), y)


def first_kernel(complete, d_hbm, rates_hbm, freqs_hbm, out_ref, w_ref, rates_ref, freqs_ref, buf, sems, psems):
    tm = lax.axis_index("tm")
    rates_copy = pltpu.make_async_copy(rates_hbm, rates_ref, psems.at[0])
    freqs_copy = pltpu.make_async_copy(freqs_hbm, freqs_ref, psems.at[1])
    rates_copy.start()
    freqs_copy.start()
    copies = load_half(d_hbm, buf, sems, 1 - half_index(tm))
    rates_copy.wait()
    freqs_copy.wait()
    count, width = buf.shape[1], out_ref.shape[1]
    steps = lax.broadcasted_iota(jnp.int32, (count, width), 0) + tm * count
    lanes = lax.broadcasted_iota(jnp.int32, (count, width), 1)
    t = steps.astype(f32) / complete
    x = decayed_waves(rates_ref[...], freqs_ref[...], t)
    x = jnp.where(lanes < width // 2, x, x * t)
    hi, lo = split(x)
    w_ref[:, :width] = hi
    w_ref[:, width:] = lo
    project(copies, buf, w_ref[...], out_ref)


def second_kernel(d_hbm, w_ref, out_ref, buf, sems):
    copies = load_half(d_hbm, buf, sems, half_index(lax.axis_index("tm")))
    project(copies, buf, w_ref[...], out_ref)


def swap_rows(x):
    rows = lax.broadcasted_iota(jnp.int32, x.shape, 0)
    n = x.shape[0]
    return jnp.where(rows % 2 == 0, pltpu.roll(x, n - 1, 0), pltpu.roll(x, 1, 0))


def swap_lanes(x):
    lanes = lax.broadcasted_iota(jnp.int32, x.shape, 1)
    n = x.shape[1]
    return jnp.where(lanes % 2 == 0, pltpu.roll(x, n - 1, 1), pltpu.roll(x, 1, 1))


def inverse_2x2(x):
    scale = 1.0 / (x[0][0] * x[1][1] - x[0][1] * x[1][0])
    return [[x[1][1] * scale, -x[0][1] * scale], [-x[1][0] * scale, x[0][0] * scale]]


def product_2x2(x, y):
    return [[x[i][0] * y[0][j] + x[i][1] * y[1][j] for j in range(2)] for i in range(2)]


def difference_2x2(x, y):
    return [[x[i][j] - y[i][j] for j in range(2)] for i in range(2)]


def inverse_4x4(m):
    a, b = [row[:2] for row in m[:2]], [row[2:] for row in m[:2]]
    c, d = [row[:2] for row in m[2:]], [row[2:] for row in m[2:]]
    ai = inverse_2x2(a)
    aib, cai = product_2x2(ai, b), product_2x2(c, ai)
    si = inverse_2x2(difference_2x2(d, product_2x2(c, aib)))
    e01 = [[-v for v in row] for row in product_2x2(aib, si)]
    e10 = [[-v for v in row] for row in product_2x2(si, cai)]
    e00 = difference_2x2(ai, product_2x2(e01, cai))
    return [e00[0] + e01[0], e00[1] + e01[1], e10[0] + si[0], e10[1] + si[1]]


def inverse(a):
    n = a.shape[0]
    rows = lax.broadcasted_iota(jnp.int32, a.shape, 0)
    lanes = lax.broadcasted_iota(jnp.int32, a.shape, 1)
    lane = lanes[:1]
    for p in range(0, n, 4):
        columns = [jnp.broadcast_to(a[:, p + i : p + i + 1], a.shape) for i in range(4)]
        pivots = [a[p + i : p + i + 1, :] for i in range(4)]
        e = inverse_4x4([[columns[j][p + i : p + i + 1] for j in range(4)] for i in range(4)])
        new = []
        for i in range(4):
            row = (e[i][0] * pivots[0] + e[i][1] * pivots[1]) + (e[i][2] * pivots[2] + e[i][3] * pivots[3])
            for j in range(4):
                row = jnp.where(lane == p + j, e[i][j], row)
            new.append(row)
        taken = (columns[0] * new[0] + columns[1] * new[1]) + (columns[2] * new[2] + columns[3] * new[3])
        a = jnp.where((lanes >= p) & (lanes < p + 4), 0.0, a) - taken
        for i in range(4):
            a = jnp.where(rows == p + i, new[i], a)
    return a


def gram_kernel(complete, rates_ref, freqs_ref, after_ref, gram_ref, slope_ref, basis_slope_ref):
    del after_ref
    width = 4 * rates_ref.shape[1]
    half = width // 2
    rates, freqs = rates_ref[...], freqs_ref[...]
    total = jnp.zeros((2 * width, 2 * width), f32)
    block = 512
    rows = lax.broadcasted_iota(jnp.int32, (block, width), 0)
    lanes = lax.broadcasted_iota(jnp.int32, (block, width), 1)
    start = jnp.where(lanes < half, rows, rows + complete // 2)
    for i in range(complete // 2 // block):
        t = (start + i * block).astype(f32) / complete
        x = decayed_waves(rates, freqs, t)
        x = jnp.concatenate([x, x * t], axis=1)
        total = total + lax.dot_general(
            x, x, (((0,), (0,)), ((), ())), precision=highest, preferred_element_type=f32
        )

    def fold(i, j):
        block = total[i * width : (i + 1) * width, j * width : (j + 1) * width]
        return block[:half] + pltpu.roll(block[half:], half, 1)

    gram_ref[...] = fold(0, 0)
    basis_slope_ref[...] = fold(0, 1)
    slope = fold(1, 1)
    lanes = lax.broadcasted_iota(jnp.int32, slope.shape, 1)
    rows = lax.broadcasted_iota(jnp.int32, slope.shape, 0)
    row_sign = jnp.where(rows % 2 == 0, -1.0, 1.0)
    lane_sign = jnp.where(lanes % 2 == 0, -1.0, 1.0)
    turned = row_sign * swap_rows(slope)
    slope_ref[0] = slope
    slope_ref[1] = lane_sign * swap_lanes(slope)
    slope_ref[2] = turned
    slope_ref[3] = lane_sign * swap_lanes(turned)


def inverse_kernel(gram_ref, after_ref, inverse_ref):
    del after_ref
    half, width = gram_ref.shape
    inv = inverse(gram_ref[...])
    inv = jnp.where(lax.broadcasted_iota(jnp.int32, inv.shape, 1) < half, inv, 0.0)
    inverse_ref[:half] = inv
    inverse_ref[half:] = pltpu.roll(inv, half, 1)


def modes_kernel(first_ref, first_in_ref, second_ref, second_in_ref, product_ref, inverse_ref, modes_ref, message_ref):
    x = jnp.concatenate([first_ref[...] + first_in_ref[...], second_ref[...] + second_in_ref[...]], axis=0)
    x = dot(x, inverse_ref[...], highest)
    count, width = x.shape
    half, quarter = width // 2, width // 4
    flat = jnp.transpose(x)
    modes_ref[:, :count] = flat[:half]
    modes_ref[:, count:] = flat[half:]
    both = dot(flat, jnp.concatenate([x, product_ref[...]], axis=1), highest)
    gram = both[:half, :width] + pltpu.roll(both[half:, :width], half, 1)
    cross = both[:half, width:] + pltpu.roll(both[half:, width:], half, 1)
    rows = lax.broadcasted_iota(jnp.int32, cross.shape, 0)
    lanes = lax.broadcasted_iota(jnp.int32, cross.shape, 1)
    even = lanes % 2 == 0
    same = jnp.sum(jnp.where(rows == lanes, cross, 0.0), axis=0, keepdims=True)
    partner = jnp.where(even, lanes + 1, lanes - 1)
    turn = jnp.sum(jnp.where(rows == partner, jnp.where(even, cross, -cross), 0.0), axis=0, keepdims=True)
    sums = jnp.where(even[:1], same + swap_lanes(same), turn + swap_lanes(turn))
    eighth, group = quarter // 2, quarter // 4
    upper = jnp.where(lanes[:eighth] < half, gram[:eighth], pltpu.roll(gram[eighth:quarter], half, 1))
    lower = jnp.zeros((group, width), f32)
    for i in range(4):
        part = gram[quarter + i * group : quarter + (i + 1) * group]
        part = pltpu.roll(part, (i * quarter - quarter) % width, 1)
        lower = jnp.where(lanes[:group] // quarter == i, part, lower)
    packed = jnp.concatenate([upper, lower], axis=0)
    y = lax.axis_index("tm") // 2
    share = packed.shape[0] // 4
    part = packed[:share]
    for i in range(1, 4):
        part = jnp.where(y == i, packed[i * share : (i + 1) * share], part)
    message_ref[...] = jnp.concatenate([part, sums, jnp.zeros((8 - share - 1, width), f32)], axis=0)


def spread_kernel(a_ref, b_ref, after_ref, out_ref):
    del after_ref
    total = a_ref[...] + b_ref[...]
    for i in range(out_ref.shape[0]):
        out_ref[i] = total


def collect_kernel(messages_ref, after_ref, out_ref):
    del after_ref
    total = messages_ref[0]
    for i in range(1, messages_ref.shape[0]):
        total = total + messages_ref[i]
    y = lax.axis_index("tm") // 2
    n = total.shape[0]
    for i in range(out_ref.shape[0] // n):
        out_ref[i * n : (i + 1) * n] = jnp.where(y == i, total, 0.0)


def misfit_kernel(d_hbm, own_ref, other_ref, w_ref, modes_hbm, misfit_hbm, done_ref, out_ref, in_sems, sems, modes_sems):
    side = half_index(lax.axis_index("tm"))
    basis, half = own_ref.shape
    width = 2 * basis
    chunks = sems.shape[0]
    rows = 2 * half // chunks
    copies = []
    for i in range(chunks):
        piece = pl.ds(i * rows, rows)
        copies.append(pltpu.make_async_copy(d_hbm.at[piece], out_ref.at[piece], in_sems.at[i]))
        copies[-1].start()
    waits = []
    for i, (ref, place) in enumerate(((own_ref, side), (other_ref, 1 - side))):
        lanes = pl.ds(pl.multiple_of(place * half, half), half)
        copy = pltpu.make_async_copy(ref, modes_hbm.at[:, lanes], modes_sems.at[i])
        copy.start()
        waits.append(copy)
    top = jnp.transpose(w_ref[:, :width].astype(f32))[:basis].astype(bf16)
    low = jnp.transpose(w_ref[:, width:].astype(f32))[:basis].astype(bf16)
    b = jnp.concatenate([top, low, top, low], axis=0)
    for i in range(chunks):
        where, start = divmod(i * rows, half)
        modes = jnp.where(side == where, own_ref[:, start : start + rows], other_ref[:, start : start + rows])
        hi, lo = split(jnp.transpose(jnp.concatenate([modes, modes], axis=0)))
        piece = pl.ds(i * rows, rows)
        fitted = dot(jnp.concatenate([hi, lo], axis=1), b)
        copies[i].wait()
        out_ref[piece, :] = out_ref[piece, :] - fitted
        copy = pltpu.make_async_copy(out_ref.at[piece], misfit_hbm.at[piece], sems.at[i])
        copy.start()
        waits.append(copy)
    for copy in waits:
        copy.wait()
    done_ref[...] = jnp.zeros_like(done_ref)


def last_kernel(divisor, a_ref, b_ref, slope_ref, basis_slope_ref, gradient_ref, newton_ref):
    total = a_ref[...] + b_ref[...]
    width = total.shape[1]
    half, quarter, eighth = width // 2, width // 4, width // 8
    share = (eighth + eighth // 2) // 4
    packed = jnp.concatenate([total[i * 8 : i * 8 + share] for i in range(4)], axis=0)
    sums = total[share : share + 1]
    for i in range(1, 4):
        sums = sums + total[i * 8 + share : i * 8 + share + 1]
    upper, lower = packed[:eighth], packed[eighth:]
    parts = [upper, pltpu.roll(upper, half, 1)]
    for i in range(4):
        parts.append(pltpu.roll(lower, (quarter - i * quarter) % width, 1))
    wide = jnp.concatenate(parts + [jnp.zeros((half, width), f32)], axis=0)
    rows = lax.broadcasted_iota(jnp.int32, (half, width), 0)
    lanes = lax.broadcasted_iota(jnp.int32, (half, width), 1)
    gram = jnp.where(rows <= lanes, wide[:half], jnp.transpose(wide)[:half])

    def block_sums(x):
        y = x + swap_rows(x)
        return y + swap_lanes(y)

    def for_row(first, second):
        return jnp.where(rows % 2 == 0, first, second)

    even = for_row(block_sums(gram * slope_ref[0]), block_sums(gram * slope_ref[2]))
    odd = for_row(block_sums(gram * slope_ref[1]), block_sums(gram * slope_ref[3]))
    newton = divisor * jnp.where(lanes % 2 == 0, even, odd)
    newton_ref[...] = newton[:, :half]
    basis_slope = basis_slope_ref[...]
    lane = lanes[:1]
    same = jnp.sum(gram * basis_slope, axis=0, keepdims=True)
    turn = jnp.sum(swap_lanes(gram) * basis_slope, axis=0, keepdims=True)
    turn = jnp.where(lane % 2 == 0, turn, -turn)
    fitted = jnp.where(lane % 2 == 0, same + swap_lanes(same), turn + swap_lanes(turn))
    gradient_ref[...] = (-divisor * (sums - fitted))[:, :half]


def flips(n, bits):
    return [(i, i ^ bits) for i in range(n)]


def cost(flops, bytes_accessed):
    return pl.CostEstimate(flops=flops, bytes_accessed=bytes_accessed, transcendentals=0)


def local(frame_slab, pair_decay_rates, pair_angular_frequencies):
    points, epochs = frame_slab.shape
    pairs = pair_decay_rates.shape[0]
    basis = 2 * pairs
    width = 2 * basis
    tm_size, space_size = lax.axis_size("tm"), lax.axis_size("space")
    complete = epochs * tm_size
    half = points // 2
    quarter = half // 2
    divisor = 1.0 / (points * space_size * complete)
    in_hbm = lambda x: pltpu.with_memory_space_constraint(x, pltpu.HBM)
    rates = in_hbm(pair_decay_rates.reshape(1, pairs))
    freqs = in_hbm(pair_angular_frequencies.reshape(1, pairs))
    slab = in_hbm(frame_slab)
    scratch = [pltpu.VMEM((half, epochs), f32), pltpu.SemaphoreType.DMA((4,))]

    away, w, rates, freqs = pl.pallas_call(
        lambda *refs: first_kernel(complete, *refs),
        out_shape=(
            jax.ShapeDtypeStruct((half, width), f32),
            jax.ShapeDtypeStruct((epochs, 2 * width), bf16),
            jax.ShapeDtypeStruct((1, pairs), f32),
            jax.ShapeDtypeStruct((1, pairs), f32),
        ),
        in_specs=[HBM, HBM, HBM],
        out_specs=(VMEM,) * 4,
        scratch_shapes=scratch + [pltpu.SemaphoreType.DMA((2,))],
        compiler_params=PARAMS,
        name="project_away",
    )(slab, rates, freqs)
    arrived = lax.ppermute(away, "tm", flips(tm_size, 1))
    kept = pl.pallas_call(
        second_kernel,
        out_shape=jax.ShapeDtypeStruct((half, width), f32),
        in_specs=[HBM, VMEM],
        out_specs=VMEM,
        scratch_shapes=scratch,
        compiler_params=PARAMS,
        cost_estimate=cost(2 * half * epochs * width * 4, half * epochs * 4),
        name="project_kept",
    )(slab, w)

    near, wrap = flips(tm_size, 3), flips(tm_size, 7)
    summed = kept + arrived
    eighth = quarter // 2
    first, second, product = summed[:eighth], summed[eighth:quarter], summed[quarter:]
    first_in = lax.ppermute(first, "tm", near)
    second_in = lax.ppermute(second, "tm", wrap)
    gram, slopes, basis_slope = pl.pallas_call(
        lambda *refs: gram_kernel(complete, *refs),
        out_shape=(
            jax.ShapeDtypeStruct((basis, width), f32),
            jax.ShapeDtypeStruct((4, basis, width), f32),
            jax.ShapeDtypeStruct((basis, width), f32),
        ),
        in_specs=[VMEM, VMEM, ANY],
        out_specs=(VMEM, VMEM, VMEM),
        compiler_params=PARAMS,
        cost_estimate=cost(10**9, 10**7),
        name="grams",
    )(rates, freqs, kept)
    first, second, gram = lax.optimization_barrier((first + first_in, second + second_in, gram))
    first_in = lax.ppermute(first, "tm", wrap)
    second_in = lax.ppermute(second, "tm", near)
    inverse_gram = pl.pallas_call(
        inverse_kernel,
        out_shape=jax.ShapeDtypeStruct((width, width), f32),
        in_specs=[VMEM, ANY],
        out_specs=VMEM,
        compiler_params=PARAMS,
        cost_estimate=cost(10**9, 10**7),
        name="inverse",
    )(gram, first)
    modes_half, message = pl.pallas_call(
        modes_kernel,
        out_shape=(
            jax.ShapeDtypeStruct((basis, half), f32),
            jax.ShapeDtypeStruct((8, width), f32),
        ),
        in_specs=[VMEM] * 6,
        out_specs=(VMEM, VMEM),
        compiler_params=PARAMS,
        name="modes",
    )(first, first_in, second, second_in, product, inverse_gram)

    message_in = lax.ppermute(message, "tm", flips(tm_size, 1))
    modes_other = lax.ppermute(modes_half, "tm", flips(tm_size, 1))
    messages = pl.pallas_call(
        spread_kernel,
        out_shape=jax.ShapeDtypeStruct((space_size, *message.shape), f32),
        in_specs=[VMEM, VMEM, ANY],
        out_specs=VMEM,
        compiler_params=PARAMS,
        name="spread",
    )(message, message_in, modes_other)
    messages = lax.all_to_all(messages, "space", 0, 0)
    blocks = 8
    spatial_modes, misfit, done = pl.pallas_call(
        misfit_kernel,
        out_shape=(
            jax.ShapeDtypeStruct((basis, points), f32),
            jax.ShapeDtypeStruct((points, epochs), f32),
            jax.ShapeDtypeStruct((8, width), f32),
        ),
        in_specs=[HBM, VMEM, VMEM, VMEM],
        out_specs=(HBM, HBM, VMEM),
        scratch_shapes=[pltpu.VMEM((points, epochs), f32)] + [pltpu.SemaphoreType.DMA((n,)) for n in (blocks, blocks, 2)],
        compiler_params=PARAMS,
        cost_estimate=cost(10**9, 10**7),
        name="misfit",
    )(slab, modes_half, modes_other, w)
    total = pl.pallas_call(
        collect_kernel,
        out_shape=jax.ShapeDtypeStruct((32, width), f32),
        in_specs=[VMEM, ANY],
        out_specs=VMEM,
        compiler_params=PARAMS,
        name="collect",
    )(messages, done)
    total = total + lax.ppermute(total, "tm", near)
    total_in = lax.ppermute(total, "tm", wrap)
    gradient, gauss_newton = pl.pallas_call(
        lambda *refs: last_kernel(divisor, *refs),
        out_shape=(
            jax.ShapeDtypeStruct((1, basis), f32),
            jax.ShapeDtypeStruct((basis, basis), f32),
        ),
        in_specs=[VMEM] * 4,
        out_specs=(VMEM, VMEM),
        compiler_params=PARAMS,
        name="newton",
    )(total, total_in, slopes, basis_slope)
    return spatial_modes, misfit, gradient.reshape(basis), gauss_newton


def solution(mesh):
    return jax.shard_map(
        local,
        mesh=mesh,
        in_specs=(P("space", "tm"), P(), P()),
        out_specs=(P(None, "space"), P("space", "tm"), P(), P()),
        check_vma=False,
    )
```

```python
import jax
import jax.numpy as jnp
from jax import lax
from jax.experimental import pallas as pl
from jax.experimental.pallas import tpu as pltpu
from jax.sharding import PartitionSpec as P

f32 = jnp.float32
bf16 = jnp.bfloat16
highest = lax.Precision.HIGHEST
VMEM = pl.BlockSpec(memory_space=pltpu.VMEM)
HBM = pl.BlockSpec(memory_space=pltpu.HBM)
ANY = pl.BlockSpec(memory_space=pl.ANY)
PARAMS = pltpu.CompilerParams(vmem_limit_bytes=40 * 1024 * 1024)


def dot(a, b, precision=None):
    return lax.dot_general(
        a, b, (((1,), (0,)), ((), ())), precision=precision, preferred_element_type=f32
    )


def dot_nt(a, b, precision=None):
    return lax.dot_general(
        a, b, (((1,), (1,)), ((), ())), precision=precision, preferred_element_type=f32
    )


def split(x):
    hi = x.astype(bf16)
    lo = (x - hi.astype(f32)).astype(bf16)
    return hi, lo


def sine_or_cosine(theta, is_cosine):
    q = jnp.floor(theta * 0.6366197723675814 + 0.5)
    r = theta - q * 1.5703125
    r = r - q * 4.837512969970703125e-4
    r = r - q * 7.5497899548918821691e-8
    s = r * r
    sine = r + r * s * (
        -0.16666666666 + s * (0.0083333293858894631756 + s * (-0.000198393348360966317347 + s * 2.7181216275479732e-6))
    )
    cosine = 1.0 + s * (
        -0.5 + s * (0.0416666641831398010253906 + s * (-0.001388833043165504932 + s * 2.4390448796277409e-5))
    )
    n = q.astype(jnp.int32) + jnp.where(is_cosine, 1, 0)
    value = jnp.where((n & 1) == 1, cosine, sine)
    return jnp.where((n & 2) == 2, -value, value)


def lane_parameters(values):
    n = values.shape[1]
    rows = lax.broadcasted_iota(jnp.int32, (n, 4 * n), 0)
    lanes = lax.broadcasted_iota(jnp.int32, (n, 4 * n), 1)
    eye = lax.broadcasted_iota(jnp.int32, (n, n), 0) == lax.broadcasted_iota(jnp.int32, (n, n), 1)
    column = jnp.sum(jnp.where(eye, values, 0.0), axis=1, keepdims=True)
    hit = (lanes % (2 * n)) // 2 == rows
    return jnp.sum(jnp.where(hit, column, 0.0), axis=0, keepdims=True)


def decayed_waves(rates, freqs, t):
    lanes = lax.broadcasted_iota(jnp.int32, t.shape, 1)
    rate = lane_parameters(rates)
    freq = lane_parameters(freqs)
    return jnp.exp(rate * t) * sine_or_cosine(freq * t, lanes % 2 == 0)


def half_index(tm):
    return (tm + tm // 2) % 2


def load_half(d_hbm, buf, sems, side):
    half = buf.shape[0]
    rows = half // sems.shape[0]
    copies = []
    for i in range(sems.shape[0]):
        piece = pl.ds(pl.multiple_of(side * half + i * rows, rows), rows)
        copies.append(pltpu.make_async_copy(d_hbm.at[piece], buf.at[pl.ds(i * rows, rows)], sems.at[i]))
        copies[-1].start()
    return copies


def project(d, w):
    width = w.shape[1] // 2
    half = width // 2
    count = d.shape[0] // 2

    def product(start):
        hi, lo = split(d[start : start + count, :])
        both = dot(hi, w) + dot(lo, w)
        return both[:, :width] + both[:, width:]

    x, y = product(0), product(count)
    left = lax.broadcasted_iota(jnp.int32, x.shape, 1) < half
    return jnp.where(left, x, pltpu.roll(y, half, 1)), jnp.where(left, pltpu.roll(x, half, 1), y)


def first_kernel(complete, d_hbm, rates_hbm, freqs_hbm, out_ref, product_ref, w_ref, rates_ref, freqs_ref, buf, sems, psems):
    tm = lax.axis_index("tm")
    rates_copy = pltpu.make_async_copy(rates_hbm, rates_ref, psems.at[0])
    freqs_copy = pltpu.make_async_copy(freqs_hbm, freqs_ref, psems.at[1])
    rates_copy.start()
    freqs_copy.start()
    copies = load_half(d_hbm, buf, sems, 1 - half_index(tm))
    rates_copy.wait()
    freqs_copy.wait()
    count, width = buf.shape[1], out_ref.shape[1]
    steps = lax.broadcasted_iota(jnp.int32, (count, width), 0) + tm * count
    lanes = lax.broadcasted_iota(jnp.int32, (count, width), 1)
    t = steps.astype(f32) / complete
    x = decayed_waves(rates_ref[...], freqs_ref[...], t)
    x = jnp.where(lanes < width // 2, x, x * t)
    hi, lo = split(x)
    w_ref[:, :width] = hi
    w_ref[:, width:] = lo
    for copy in copies:
        copy.wait()
    projection, product = project(buf, w_ref[...])
    out_ref[...] = projection
    product_ref[...] = product


def second_kernel(d_ref, w_ref, first_ref, second_ref, product_ref):
    half = d_ref.shape[0] // 2
    start = half_index(lax.axis_index("tm")) * half
    projection, product = project(d_ref.at[pl.ds(pl.multiple_of(start, half), half)], w_ref[...])
    count = first_ref.shape[0]
    first_ref[...] = projection[:count]
    second_ref[...] = projection[count:]
    product_ref[...] = product


def swap_rows(x):
    rows = lax.broadcasted_iota(jnp.int32, x.shape, 0)
    n = x.shape[0]
    return jnp.where(rows % 2 == 0, pltpu.roll(x, n - 1, 0), pltpu.roll(x, 1, 0))


def swap_lanes(x):
    lanes = lax.broadcasted_iota(jnp.int32, x.shape, 1)
    n = x.shape[1]
    return jnp.where(lanes % 2 == 0, pltpu.roll(x, n - 1, 1), pltpu.roll(x, 1, 1))


def inverse_2x2(x):
    scale = 1.0 / (x[0][0] * x[1][1] - x[0][1] * x[1][0])
    return [[x[1][1] * scale, -x[0][1] * scale], [-x[1][0] * scale, x[0][0] * scale]]


def product_2x2(x, y):
    return [[x[i][0] * y[0][j] + x[i][1] * y[1][j] for j in range(2)] for i in range(2)]


def difference_2x2(x, y):
    return [[x[i][j] - y[i][j] for j in range(2)] for i in range(2)]


def inverse_4x4(m):
    a, b = [row[:2] for row in m[:2]], [row[2:] for row in m[:2]]
    c, d = [row[:2] for row in m[2:]], [row[2:] for row in m[2:]]
    ai = inverse_2x2(a)
    aib, cai = product_2x2(ai, b), product_2x2(c, ai)
    si = inverse_2x2(difference_2x2(d, product_2x2(c, aib)))
    e01 = [[-v for v in row] for row in product_2x2(aib, si)]
    e10 = [[-v for v in row] for row in product_2x2(si, cai)]
    e00 = difference_2x2(ai, product_2x2(e01, cai))
    return [e00[0] + e01[0], e00[1] + e01[1], e10[0] + si[0], e10[1] + si[1]]


def inverse(a):
    n = a.shape[0]
    rows = lax.broadcasted_iota(jnp.int32, a.shape, 0)
    lanes = lax.broadcasted_iota(jnp.int32, a.shape, 1)
    lane = lanes[:1]
    for p in range(0, n, 4):
        columns = [jnp.broadcast_to(a[:, p + i : p + i + 1], a.shape) for i in range(4)]
        pivots = [a[p + i : p + i + 1, :] for i in range(4)]
        e = inverse_4x4([[columns[j][p + i : p + i + 1] for j in range(4)] for i in range(4)])
        new = []
        for i in range(4):
            row = (e[i][0] * pivots[0] + e[i][1] * pivots[1]) + (e[i][2] * pivots[2] + e[i][3] * pivots[3])
            for j in range(4):
                row = jnp.where(lane == p + j, e[i][j], row)
            new.append(row)
        taken = (columns[0] * new[0] + columns[1] * new[1]) + (columns[2] * new[2] + columns[3] * new[3])
        a = jnp.where((lanes >= p) & (lanes < p + 4), 0.0, a) - taken
        for i in range(4):
            a = jnp.where(rows == p + i, new[i], a)
    return a


def dot_tn(a, b):
    return lax.dot_general(a, b, (((0,), (0,)), ((), ())), preferred_element_type=f32)


def gram_kernel(complete, rates_ref, freqs_ref, after_ref, gram_ref, slope_ref, basis_slope_ref):
    del after_ref
    width = 4 * rates_ref.shape[1]
    half = width // 2
    rates, freqs = rates_ref[...], freqs_ref[...]
    with_basis = jnp.zeros((2 * width, 4 * width), f32)
    with_slope = jnp.zeros((2 * width, 2 * width), f32)
    block = 512
    rows = lax.broadcasted_iota(jnp.int32, (block, width), 0)
    lanes = lax.broadcasted_iota(jnp.int32, (block, width), 1)
    start = jnp.where(lanes < half, rows, rows + complete // 2)
    for i in range(complete // 2 // block):
        t = (start + i * block).astype(f32) / complete
        x = decayed_waves(rates, freqs, t)
        z = jnp.concatenate([*split(x), *split(x * t)], axis=1)
        with_basis = with_basis + dot_tn(z[:, : 2 * width], z)
        with_slope = with_slope + dot_tn(z[:, 2 * width :], z[:, 2 * width :])

    def fold(total, j):
        block = total[:, j : j + width] + total[:, j + width : j + 2 * width]
        block = block[:width] + block[width:]
        return block[:half] + pltpu.roll(block[half:], half, 1)

    gram_ref[...] = fold(with_basis, 0)
    basis_slope_ref[...] = fold(with_basis, 2 * width)
    slope = fold(with_slope, 0)
    lanes = lax.broadcasted_iota(jnp.int32, slope.shape, 1)
    rows = lax.broadcasted_iota(jnp.int32, slope.shape, 0)
    row_sign = jnp.where(rows % 2 == 0, -1.0, 1.0)
    lane_sign = jnp.where(lanes % 2 == 0, -1.0, 1.0)
    turned = row_sign * swap_rows(slope)
    slope_ref[0] = slope
    slope_ref[1] = lane_sign * swap_lanes(slope)
    slope_ref[2] = turned
    slope_ref[3] = lane_sign * swap_lanes(turned)


def inverse_kernel(gram_ref, after_ref, inverse_ref):
    del after_ref
    half, width = gram_ref.shape
    inv = inverse(gram_ref[...])
    inv = jnp.where(lax.broadcasted_iota(jnp.int32, inv.shape, 1) < half, inv, 0.0)
    inv = jnp.concatenate([inv, pltpu.roll(inv, half, 1)], axis=0)
    one, two = split(inv)
    three = (inv - one.astype(f32) - two.astype(f32)).astype(bf16)
    twice = jnp.concatenate([one, two], axis=1)
    inverse_ref[:width] = twice
    inverse_ref[width : 2 * width] = twice
    inverse_ref[2 * width :] = jnp.concatenate([three, jnp.zeros_like(three)], axis=1)


def modes_kernel(first_ref, first_in_ref, second_ref, second_in_ref, product_ref, product_in_ref, inverse_ref, modes_ref, message_ref):
    x = jnp.concatenate([first_ref[...] + first_in_ref[...], second_ref[...] + second_in_ref[...]], axis=0)
    width = x.shape[1]
    hi, lo = split(x)
    both = dot(jnp.concatenate([hi, lo], axis=1), inverse_ref[: 2 * width])
    x = both[:, :width] + (both[:, width:] + dot(hi, inverse_ref[2 * width :, :width]))
    count = x.shape[0]
    half, quarter = width // 2, width // 4
    flat = jnp.transpose(x)
    modes_ref[:, :count] = flat[:half]
    modes_ref[:, count:] = flat[half:]
    both = dot(flat, jnp.concatenate([x, product_ref[...] + product_in_ref[...]], axis=1), highest)
    gram = both[:half, :width] + pltpu.roll(both[half:, :width], half, 1)
    cross = both[:half, width:] + pltpu.roll(both[half:, width:], half, 1)
    rows = lax.broadcasted_iota(jnp.int32, cross.shape, 0)
    lanes = lax.broadcasted_iota(jnp.int32, cross.shape, 1)
    even = lanes % 2 == 0
    same = jnp.sum(jnp.where(rows == lanes, cross, 0.0), axis=0, keepdims=True)
    partner = jnp.where(even, lanes + 1, lanes - 1)
    turn = jnp.sum(jnp.where(rows == partner, jnp.where(even, cross, -cross), 0.0), axis=0, keepdims=True)
    sums = jnp.where(even[:1], same + swap_lanes(same), turn + swap_lanes(turn))
    eighth, group = quarter // 2, quarter // 4
    upper = jnp.where(lanes[:eighth] < half, gram[:eighth], pltpu.roll(gram[eighth:quarter], half, 1))
    lower = jnp.zeros((group, width), f32)
    for i in range(4):
        part = gram[quarter + i * group : quarter + (i + 1) * group]
        part = pltpu.roll(part, (i * quarter - quarter) % width, 1)
        lower = jnp.where(lanes[:group] // quarter == i, part, lower)
    packed = jnp.concatenate([upper, lower], axis=0)
    y = lax.axis_index("tm") // 2
    share = packed.shape[0] // 4
    part = packed[:share]
    for i in range(1, 4):
        part = jnp.where(y == i, packed[i * share : (i + 1) * share], part)
    message_ref[...] = jnp.concatenate([part, sums, jnp.zeros((8 - share - 1, width), f32)], axis=0)


def spread_kernel(a_ref, b_ref, after_ref, out_ref):
    del after_ref
    total = a_ref[...] + b_ref[...]
    for i in range(out_ref.shape[0]):
        out_ref[i] = total


def collect_kernel(messages_ref, after_ref, out_ref):
    del after_ref
    total = messages_ref[0]
    for i in range(1, messages_ref.shape[0]):
        total = total + messages_ref[i]
    y = lax.axis_index("tm") // 2
    n = total.shape[0]
    for i in range(out_ref.shape[0] // n):
        out_ref[i * n : (i + 1) * n] = jnp.where(y == i, total, 0.0)


def misfit_kernel(d_hbm, own_ref, other_ref, w_ref, modes_hbm, misfit_hbm, done_ref, out_ref, in_sems, sems, modes_sems):
    side = half_index(lax.axis_index("tm"))
    basis, half = own_ref.shape
    width = 2 * basis
    chunks = sems.shape[0]
    rows = 2 * half // chunks
    copies = []
    for i in range(chunks):
        piece = pl.ds(i * rows, rows)
        copies.append(pltpu.make_async_copy(d_hbm.at[piece], out_ref.at[piece], in_sems.at[i]))
        copies[-1].start()
    waits = []
    for i, (ref, place) in enumerate(((own_ref, side), (other_ref, 1 - side))):
        lanes = pl.ds(pl.multiple_of(place * half, half), half)
        copy = pltpu.make_async_copy(ref, modes_hbm.at[:, lanes], modes_sems.at[i])
        copy.start()
        waits.append(copy)
    top = jnp.transpose(w_ref[:, :width].astype(f32))[:basis].astype(bf16)
    low = jnp.transpose(w_ref[:, width:].astype(f32))[:basis].astype(bf16)
    b = jnp.concatenate([top, low, top, low], axis=0)
    for i in range(chunks):
        where, start = divmod(i * rows, half)
        modes = jnp.where(side == where, own_ref[:, start : start + rows], other_ref[:, start : start + rows])
        hi, lo = split(jnp.transpose(jnp.concatenate([modes, modes], axis=0)))
        piece = pl.ds(i * rows, rows)
        fitted = dot(jnp.concatenate([hi, lo], axis=1), b)
        copies[i].wait()
        out_ref[piece, :] = out_ref[piece, :] - fitted
        copy = pltpu.make_async_copy(out_ref.at[piece], misfit_hbm.at[piece], sems.at[i])
        copy.start()
        waits.append(copy)
    for copy in waits:
        copy.wait()
    done_ref[...] = jnp.zeros_like(done_ref)


def last_kernel(divisor, a_ref, b_ref, slope_ref, basis_slope_ref, gradient_ref, newton_ref):
    total = a_ref[...] + b_ref[...]
    width = total.shape[1]
    half, quarter, eighth = width // 2, width // 4, width // 8
    share = (eighth + eighth // 2) // 4
    packed = jnp.concatenate([total[i * 8 : i * 8 + share] for i in range(4)], axis=0)
    sums = total[share : share + 1]
    for i in range(1, 4):
        sums = sums + total[i * 8 + share : i * 8 + share + 1]
    upper, lower = packed[:eighth], packed[eighth:]
    parts = [upper, pltpu.roll(upper, half, 1)]
    for i in range(4):
        parts.append(pltpu.roll(lower, (quarter - i * quarter) % width, 1))
    wide = jnp.concatenate(parts + [jnp.zeros((half, width), f32)], axis=0)
    rows = lax.broadcasted_iota(jnp.int32, (half, width), 0)
    lanes = lax.broadcasted_iota(jnp.int32, (half, width), 1)
    gram = jnp.where(rows <= lanes, wide[:half], jnp.transpose(wide)[:half])

    def block_sums(x):
        y = x + swap_rows(x)
        return y + swap_lanes(y)

    def for_row(first, second):
        return jnp.where(rows % 2 == 0, first, second)

    even = for_row(block_sums(gram * slope_ref[0]), block_sums(gram * slope_ref[2]))
    odd = for_row(block_sums(gram * slope_ref[1]), block_sums(gram * slope_ref[3]))
    newton = divisor * jnp.where(lanes % 2 == 0, even, odd)
    newton_ref[...] = newton[:, :half]
    basis_slope = basis_slope_ref[...]
    lane = lanes[:1]
    same = jnp.sum(gram * basis_slope, axis=0, keepdims=True)
    turn = jnp.sum(swap_lanes(gram) * basis_slope, axis=0, keepdims=True)
    turn = jnp.where(lane % 2 == 0, turn, -turn)
    fitted = jnp.where(lane % 2 == 0, same + swap_lanes(same), turn + swap_lanes(turn))
    gradient_ref[...] = (-divisor * (sums - fitted))[:, :half]


def flips(n, bits):
    return [(i, i ^ bits) for i in range(n)]


def cost(flops, bytes_accessed):
    return pl.CostEstimate(flops=flops, bytes_accessed=bytes_accessed, transcendentals=0)


def local(frame_slab, pair_decay_rates, pair_angular_frequencies):
    points, epochs = frame_slab.shape
    pairs = pair_decay_rates.shape[0]
    basis = 2 * pairs
    width = 2 * basis
    tm_size, space_size = lax.axis_size("tm"), lax.axis_size("space")
    complete = epochs * tm_size
    half = points // 2
    quarter = half // 2
    divisor = 1.0 / (points * space_size * complete)
    in_hbm = lambda x: pltpu.with_memory_space_constraint(x, pltpu.HBM)
    rates = in_hbm(pair_decay_rates.reshape(1, pairs))
    freqs = in_hbm(pair_angular_frequencies.reshape(1, pairs))
    slab = in_hbm(frame_slab)
    scratch = [pltpu.VMEM((half, epochs), f32), pltpu.SemaphoreType.DMA((4,))]

    away, product_away, w, rates, freqs = pl.pallas_call(
        lambda *refs: first_kernel(complete, *refs),
        out_shape=(
            jax.ShapeDtypeStruct((quarter, width), f32),
            jax.ShapeDtypeStruct((quarter, width), f32),
            jax.ShapeDtypeStruct((epochs, 2 * width), bf16),
            jax.ShapeDtypeStruct((1, pairs), f32),
            jax.ShapeDtypeStruct((1, pairs), f32),
        ),
        in_specs=[HBM, HBM, HBM],
        out_specs=(VMEM,) * 5,
        scratch_shapes=scratch + [pltpu.SemaphoreType.DMA((2,))],
        compiler_params=PARAMS,
        name="project_away",
    )(slab, rates, freqs)
    arrived = lax.ppermute(away, "tm", flips(tm_size, 1))
    eighth = quarter // 2
    first, second, product = pl.pallas_call(
        second_kernel,
        out_shape=[jax.ShapeDtypeStruct((n, width), f32) for n in (eighth, eighth, quarter)],
        in_specs=[VMEM, VMEM],
        out_specs=[VMEM] * 3,
        compiler_params=PARAMS,
        cost_estimate=cost(2 * half * epochs * width * 4, half * epochs * 4),
        name="project_kept",
    )(frame_slab, w)

    near, wrap = flips(tm_size, 3), flips(tm_size, 7)
    first, second = first + arrived[:eighth], second + arrived[eighth:]
    product_away, first, second = lax.optimization_barrier((product_away, first, second))
    product_in = lax.ppermute(product_away, "tm", flips(tm_size, 1))
    first_in = lax.ppermute(first, "tm", near)
    second_in = lax.ppermute(second, "tm", wrap)
    gram, slopes, basis_slope = pl.pallas_call(
        lambda *refs: gram_kernel(complete, *refs),
        out_shape=(
            jax.ShapeDtypeStruct((basis, width), f32),
            jax.ShapeDtypeStruct((4, basis, width), f32),
            jax.ShapeDtypeStruct((basis, width), f32),
        ),
        in_specs=[VMEM, VMEM, ANY],
        out_specs=(VMEM, VMEM, VMEM),
        compiler_params=PARAMS,
        cost_estimate=cost(10**9, 10**7),
        name="grams",
    )(rates, freqs, product)
    first, gram = lax.optimization_barrier((first + first_in, gram))
    first_in = lax.ppermute(first, "tm", wrap)
    second, first = lax.optimization_barrier((second, first))
    second = second + second_in
    second_in = lax.ppermute(second, "tm", near)
    inverse_gram = pl.pallas_call(
        inverse_kernel,
        out_shape=jax.ShapeDtypeStruct((3 * width, 2 * width), bf16),
        in_specs=[VMEM, ANY],
        out_specs=VMEM,
        compiler_params=PARAMS,
        cost_estimate=cost(10**9, 10**7),
        name="inverse",
    )(gram, second)
    modes_half, message = pl.pallas_call(
        modes_kernel,
        out_shape=(
            jax.ShapeDtypeStruct((basis, half), f32),
            jax.ShapeDtypeStruct((8, width), f32),
        ),
        in_specs=[VMEM] * 7,
        out_specs=(VMEM, VMEM),
        compiler_params=PARAMS,
        name="modes",
    )(first, first_in, second, second_in, product, product_in, inverse_gram)

    message_in = lax.ppermute(message, "tm", flips(tm_size, 1))
    modes_other = lax.ppermute(modes_half, "tm", flips(tm_size, 1))
    messages = pl.pallas_call(
        spread_kernel,
        out_shape=jax.ShapeDtypeStruct((space_size, *message.shape), f32),
        in_specs=[VMEM, VMEM, ANY],
        out_specs=VMEM,
        compiler_params=PARAMS,
        name="spread",
    )(message, message_in, modes_other)
    messages = lax.all_to_all(messages, "space", 0, 0, axis_index_groups=[list(range(space_size))[::-1]])
    blocks = 8
    spatial_modes, misfit, done = pl.pallas_call(
        misfit_kernel,
        out_shape=(
            jax.ShapeDtypeStruct((basis, points), f32),
            jax.ShapeDtypeStruct((points, epochs), f32),
            jax.ShapeDtypeStruct((8, width), f32),
        ),
        in_specs=[HBM, VMEM, VMEM, VMEM],
        out_specs=(HBM, HBM, VMEM),
        scratch_shapes=[pltpu.VMEM((points, epochs), f32)] + [pltpu.SemaphoreType.DMA((n,)) for n in (blocks, blocks, 2)],
        compiler_params=PARAMS,
        cost_estimate=cost(10**9, 10**7),
        name="misfit",
    )(slab, modes_half, modes_other, w)
    total = pl.pallas_call(
        collect_kernel,
        out_shape=jax.ShapeDtypeStruct((32, width), f32),
        in_specs=[VMEM, ANY],
        out_specs=VMEM,
        compiler_params=PARAMS,
        name="collect",
    )(messages, done)
    total = total + lax.ppermute(total, "tm", near)
    total_in = lax.ppermute(total, "tm", wrap)
    gradient, gauss_newton = pl.pallas_call(
        lambda *refs: last_kernel(divisor, *refs),
        out_shape=(
            jax.ShapeDtypeStruct((1, basis), f32),
            jax.ShapeDtypeStruct((basis, basis), f32),
        ),
        in_specs=[VMEM] * 4,
        out_specs=(VMEM, VMEM),
        compiler_params=PARAMS,
        name="newton",
    )(total, total_in, slopes, basis_slope)
    return spatial_modes, misfit, gradient.reshape(basis), gauss_newton


def solution(mesh):
    return jax.shard_map(
        local,
        mesh=mesh,
        in_specs=(P("space", "tm"), P(), P()),
        out_specs=(P(None, "space"), P("space", "tm"), P(), P()),
        check_vma=False,
    )
```

```python
import jax
import jax.numpy as jnp
from jax import lax
from jax.experimental import pallas as pl
from jax.experimental.pallas import tpu as pltpu
from jax.sharding import PartitionSpec as P

f32 = jnp.float32
bf16 = jnp.bfloat16
highest = lax.Precision.HIGHEST
VMEM = pl.BlockSpec(memory_space=pltpu.VMEM)
HBM = pl.BlockSpec(memory_space=pltpu.HBM)
ANY = pl.BlockSpec(memory_space=pl.ANY)
PARAMS = pltpu.CompilerParams(vmem_limit_bytes=40 * 1024 * 1024)


def dot(a, b, precision=None):
    return lax.dot_general(
        a, b, (((1,), (0,)), ((), ())), precision=precision, preferred_element_type=f32
    )


def dot_nt(a, b, precision=None):
    return lax.dot_general(
        a, b, (((1,), (1,)), ((), ())), precision=precision, preferred_element_type=f32
    )


def split(x):
    hi = x.astype(bf16)
    lo = (x - hi.astype(f32)).astype(bf16)
    return hi, lo


def sine_or_cosine(theta, is_cosine):
    q = jnp.floor(theta * 0.6366197723675814 + 0.5)
    r = theta - q * 1.5703125
    r = r - q * 4.837512969970703125e-4
    r = r - q * 7.5497899548918821691e-8
    s = r * r
    sine = r + r * s * (
        -0.16666666666 + s * (0.0083333293858894631756 + s * (-0.000198393348360966317347 + s * 2.7181216275479732e-6))
    )
    cosine = 1.0 + s * (
        -0.5 + s * (0.0416666641831398010253906 + s * (-0.001388833043165504932 + s * 2.4390448796277409e-5))
    )
    n = q.astype(jnp.int32) + jnp.where(is_cosine, 1, 0)
    value = jnp.where((n & 1) == 1, cosine, sine)
    return jnp.where((n & 2) == 2, -value, value)


def lane_parameters(values):
    n = values.shape[1]
    rows = lax.broadcasted_iota(jnp.int32, (n, 4 * n), 0)
    lanes = lax.broadcasted_iota(jnp.int32, (n, 4 * n), 1)
    eye = lax.broadcasted_iota(jnp.int32, (n, n), 0) == lax.broadcasted_iota(jnp.int32, (n, n), 1)
    column = jnp.sum(jnp.where(eye, values, 0.0), axis=1, keepdims=True)
    hit = (lanes % (2 * n)) // 2 == rows
    return jnp.sum(jnp.where(hit, column, 0.0), axis=0, keepdims=True)


def decayed_waves(rates, freqs, t):
    lanes = lax.broadcasted_iota(jnp.int32, t.shape, 1)
    rate = lane_parameters(rates)
    freq = lane_parameters(freqs)
    return jnp.exp(rate * t) * sine_or_cosine(freq * t, lanes % 2 == 0)


def half_index(tm):
    return (tm + tm // 2) % 2


def load_half(d_hbm, buf, sems, side):
    half = buf.shape[0]
    rows = half // sems.shape[0]
    copies = []
    for i in range(sems.shape[0]):
        piece = pl.ds(pl.multiple_of(side * half + i * rows, rows), rows)
        copies.append(pltpu.make_async_copy(d_hbm.at[piece], buf.at[pl.ds(i * rows, rows)], sems.at[i]))
        copies[-1].start()
    return copies


def project(d, w):
    width = w.shape[1] // 2
    half = width // 2
    count = d.shape[0] // 2

    def product(start):
        hi, lo = split(d[start : start + count, :])
        both = dot(hi, w) + dot(lo, w)
        return both[:, :width] + both[:, width:]

    x, y = product(0), product(count)
    left = lax.broadcasted_iota(jnp.int32, x.shape, 1) < half
    return jnp.where(left, x, pltpu.roll(y, half, 1)), jnp.where(left, pltpu.roll(x, half, 1), y)


def first_kernel(complete, d_hbm, rates_hbm, freqs_hbm, out_ref, product_ref, w_ref, rates_ref, freqs_ref, buf, sems, psems):
    tm = lax.axis_index("tm")
    rates_copy = pltpu.make_async_copy(rates_hbm, rates_ref, psems.at[0])
    freqs_copy = pltpu.make_async_copy(freqs_hbm, freqs_ref, psems.at[1])
    rates_copy.start()
    freqs_copy.start()
    copies = load_half(d_hbm, buf, sems, 1 - half_index(tm))
    rates_copy.wait()
    freqs_copy.wait()
    count, width = buf.shape[1], out_ref.shape[1]
    steps = lax.broadcasted_iota(jnp.int32, (count, width), 0) + tm * count
    lanes = lax.broadcasted_iota(jnp.int32, (count, width), 1)
    t = steps.astype(f32) / complete
    x = decayed_waves(rates_ref[...], freqs_ref[...], t)
    x = jnp.where(lanes < width // 2, x, x * t)
    hi, lo = split(x)
    w_ref[:, :width] = hi
    w_ref[:, width:] = lo
    for copy in copies:
        copy.wait()
    projection, product = project(buf, w_ref[...])
    out_ref[...] = projection
    product_ref[...] = product


def second_kernel(d_ref, w_ref, first_ref, second_ref, product_ref):
    half = d_ref.shape[0] // 2
    start = half_index(lax.axis_index("tm")) * half
    projection, product = project(d_ref.at[pl.ds(pl.multiple_of(start, half), half)], w_ref[...])
    count = first_ref.shape[0]
    first_ref[...] = projection[:count]
    second_ref[...] = projection[count:]
    product_ref[...] = product


def swap_rows(x):
    rows = lax.broadcasted_iota(jnp.int32, x.shape, 0)
    n = x.shape[0]
    return jnp.where(rows % 2 == 0, pltpu.roll(x, n - 1, 0), pltpu.roll(x, 1, 0))


def swap_lanes(x):
    lanes = lax.broadcasted_iota(jnp.int32, x.shape, 1)
    n = x.shape[1]
    return jnp.where(lanes % 2 == 0, pltpu.roll(x, n - 1, 1), pltpu.roll(x, 1, 1))


def inverse_2x2(x):
    scale = 1.0 / (x[0][0] * x[1][1] - x[0][1] * x[1][0])
    return [[x[1][1] * scale, -x[0][1] * scale], [-x[1][0] * scale, x[0][0] * scale]]


def product_2x2(x, y):
    return [[x[i][0] * y[0][j] + x[i][1] * y[1][j] for j in range(2)] for i in range(2)]


def difference_2x2(x, y):
    return [[x[i][j] - y[i][j] for j in range(2)] for i in range(2)]


def inverse_4x4(m):
    a, b = [row[:2] for row in m[:2]], [row[2:] for row in m[:2]]
    c, d = [row[:2] for row in m[2:]], [row[2:] for row in m[2:]]
    ai = inverse_2x2(a)
    aib, cai = product_2x2(ai, b), product_2x2(c, ai)
    si = inverse_2x2(difference_2x2(d, product_2x2(c, aib)))
    e01 = [[-v for v in row] for row in product_2x2(aib, si)]
    e10 = [[-v for v in row] for row in product_2x2(si, cai)]
    e00 = difference_2x2(ai, product_2x2(e01, cai))
    return [e00[0] + e01[0], e00[1] + e01[1], e10[0] + si[0], e10[1] + si[1]]


def inverse(a):
    n = a.shape[0]
    rows = lax.broadcasted_iota(jnp.int32, a.shape, 0)
    lanes = lax.broadcasted_iota(jnp.int32, a.shape, 1)
    lane = lanes[:1]
    for p in range(0, n, 4):
        columns = [jnp.broadcast_to(a[:, p + i : p + i + 1], a.shape) for i in range(4)]
        pivots = [a[p + i : p + i + 1, :] for i in range(4)]
        e = inverse_4x4([[columns[j][p + i : p + i + 1] for j in range(4)] for i in range(4)])
        new = []
        for i in range(4):
            row = (e[i][0] * pivots[0] + e[i][1] * pivots[1]) + (e[i][2] * pivots[2] + e[i][3] * pivots[3])
            for j in range(4):
                row = jnp.where(lane == p + j, e[i][j], row)
            new.append(row)
        taken = (columns[0] * new[0] + columns[1] * new[1]) + (columns[2] * new[2] + columns[3] * new[3])
        a = jnp.where((lanes >= p) & (lanes < p + 4), 0.0, a) - taken
        for i in range(4):
            a = jnp.where(rows == p + i, new[i], a)
    return a


def dot_tn(a, b):
    return lax.dot_general(a, b, (((0,), (0,)), ((), ())), preferred_element_type=f32)


def gram_kernel(complete, rates_ref, freqs_ref, after_ref, gram_ref, slope_ref, basis_slope_ref):
    del after_ref
    width = 4 * rates_ref.shape[1]
    half = width // 2
    rates, freqs = rates_ref[...], freqs_ref[...]
    with_basis = jnp.zeros((2 * width, 4 * width), f32)
    with_slope = jnp.zeros((2 * width, 2 * width), f32)
    block = 512
    rows = lax.broadcasted_iota(jnp.int32, (block, width), 0)
    lanes = lax.broadcasted_iota(jnp.int32, (block, width), 1)
    start = jnp.where(lanes < half, rows, rows + complete // 2)
    for i in range(complete // 2 // block):
        t = (start + i * block).astype(f32) / complete
        x = decayed_waves(rates, freqs, t)
        z = jnp.concatenate([*split(x), *split(x * t)], axis=1)
        with_basis = with_basis + dot_tn(z[:, : 2 * width], z)
        with_slope = with_slope + dot_tn(z[:, 2 * width :], z[:, 2 * width :])

    def fold(total, j):
        block = total[:, j : j + width] + total[:, j + width : j + 2 * width]
        block = block[:width] + block[width:]
        return block[:half] + pltpu.roll(block[half:], half, 1)

    gram_ref[...] = fold(with_basis, 0)
    basis_slope_ref[...] = fold(with_basis, 2 * width)
    slope = fold(with_slope, 0)
    lanes = lax.broadcasted_iota(jnp.int32, slope.shape, 1)
    rows = lax.broadcasted_iota(jnp.int32, slope.shape, 0)
    row_sign = jnp.where(rows % 2 == 0, -1.0, 1.0)
    lane_sign = jnp.where(lanes % 2 == 0, -1.0, 1.0)
    turned = row_sign * swap_rows(slope)
    slope_ref[0] = slope
    slope_ref[1] = lane_sign * swap_lanes(slope)
    slope_ref[2] = turned
    slope_ref[3] = lane_sign * swap_lanes(turned)


def inverse_kernel(gram_ref, after_ref, inverse_ref):
    del after_ref
    half, width = gram_ref.shape
    inv = inverse(gram_ref[...])
    inv = jnp.where(lax.broadcasted_iota(jnp.int32, inv.shape, 1) < half, inv, 0.0)
    inv = jnp.concatenate([inv, pltpu.roll(inv, half, 1)], axis=0)
    one, two = split(inv)
    three = (inv - one.astype(f32) - two.astype(f32)).astype(bf16)
    twice = jnp.concatenate([one, two], axis=1)
    inverse_ref[:width] = twice
    inverse_ref[width : 2 * width] = twice
    inverse_ref[2 * width :] = jnp.concatenate([three, jnp.zeros_like(three)], axis=1)


def modes_kernel(first_ref, first_in_ref, second_ref, second_in_ref, product_ref, product_in_ref, inverse_ref, modes_ref, message_ref):
    x = jnp.concatenate([first_ref[...] + first_in_ref[...], second_ref[...] + second_in_ref[...]], axis=0)
    width = x.shape[1]
    hi, lo = split(x)
    both = dot(jnp.concatenate([hi, lo], axis=1), inverse_ref[: 2 * width])
    x = both[:, :width] + (both[:, width:] + dot(hi, inverse_ref[2 * width :, :width]))
    count = x.shape[0]
    half, quarter = width // 2, width // 4
    flat = jnp.transpose(x)
    modes_ref[:, :count] = flat[:half]
    modes_ref[:, count:] = flat[half:]
    both = dot(flat, jnp.concatenate([x, product_ref[...] + product_in_ref[...]], axis=1), highest)
    gram = both[:half, :width] + pltpu.roll(both[half:, :width], half, 1)
    cross = both[:half, width:] + pltpu.roll(both[half:, width:], half, 1)
    rows = lax.broadcasted_iota(jnp.int32, cross.shape, 0)
    lanes = lax.broadcasted_iota(jnp.int32, cross.shape, 1)
    even = lanes % 2 == 0
    same = jnp.sum(jnp.where(rows == lanes, cross, 0.0), axis=0, keepdims=True)
    partner = jnp.where(even, lanes + 1, lanes - 1)
    turn = jnp.sum(jnp.where(rows == partner, jnp.where(even, cross, -cross), 0.0), axis=0, keepdims=True)
    sums = jnp.where(even[:1], same + swap_lanes(same), turn + swap_lanes(turn))
    eighth, group = quarter // 2, quarter // 4
    upper = jnp.where(lanes[:eighth] < half, gram[:eighth], pltpu.roll(gram[eighth:quarter], half, 1))
    lower = jnp.zeros((group, width), f32)
    for i in range(4):
        part = gram[quarter + i * group : quarter + (i + 1) * group]
        part = pltpu.roll(part, (i * quarter - quarter) % width, 1)
        lower = jnp.where(lanes[:group] // quarter == i, part, lower)
    packed = jnp.concatenate([upper, lower], axis=0)
    y = lax.axis_index("tm") // 2
    share = packed.shape[0] // 4
    part = packed[:share]
    for i in range(1, 4):
        part = jnp.where(y == i, packed[i * share : (i + 1) * share], part)
    message_ref[...] = jnp.concatenate([part, sums, jnp.zeros((8 - share - 1, width), f32)], axis=0)


def spread_kernel(a_ref, b_ref, after_ref, out_ref):
    del after_ref
    total = a_ref[...] + b_ref[...]
    for i in range(out_ref.shape[0]):
        out_ref[i] = total


def collect_kernel(messages_ref, after_ref, out_ref):
    del after_ref
    total = messages_ref[0]
    for i in range(1, messages_ref.shape[0]):
        total = total + messages_ref[i]
    out_ref[...] = total


def misfit_kernel(d_hbm, own_ref, other_ref, w_ref, modes_hbm, misfit_hbm, done_ref, out_ref, in_sems, sems, modes_sems):
    side = half_index(lax.axis_index("tm"))
    basis, half = own_ref.shape
    width = 2 * basis
    chunks = sems.shape[0]
    rows = 2 * half // chunks
    copies = []
    for i in range(chunks):
        piece = pl.ds(i * rows, rows)
        copies.append(pltpu.make_async_copy(d_hbm.at[piece], out_ref.at[piece], in_sems.at[i]))
        copies[-1].start()
    waits = []
    for i, (ref, place) in enumerate(((own_ref, side), (other_ref, 1 - side))):
        lanes = pl.ds(pl.multiple_of(place * half, half), half)
        copy = pltpu.make_async_copy(ref, modes_hbm.at[:, lanes], modes_sems.at[i])
        copy.start()
        waits.append(copy)
    top = jnp.transpose(w_ref[:, :width].astype(f32))[:basis].astype(bf16)
    low = jnp.transpose(w_ref[:, width:].astype(f32))[:basis].astype(bf16)
    b = jnp.concatenate([top, low, top, low], axis=0)
    for i in range(chunks):
        where, start = divmod(i * rows, half)
        modes = jnp.where(side == where, own_ref[:, start : start + rows], other_ref[:, start : start + rows])
        hi, lo = split(jnp.transpose(jnp.concatenate([modes, modes], axis=0)))
        piece = pl.ds(i * rows, rows)
        fitted = dot(jnp.concatenate([hi, lo], axis=1), b)
        copies[i].wait()
        out_ref[piece, :] = out_ref[piece, :] - fitted
        copy = pltpu.make_async_copy(out_ref.at[piece], misfit_hbm.at[piece], sems.at[i])
        copy.start()
        waits.append(copy)
    for copy in waits:
        copy.wait()
    done_ref[...] = jnp.zeros_like(done_ref)


def last_kernel(divisor, own_ref, near_ref, far_ref, slope_ref, basis_slope_ref, gradient_ref, newton_ref):
    y = lax.axis_index("tm") // 2
    n = own_ref.shape[0]
    shares = [(0, own_ref[...]), (1, near_ref[...]), (3, far_ref[:n]), (2, far_ref[n:])]
    tiles = []
    for i in range(4):
        tile = shares[0][1]
        for offset, share in shares[1:]:
            tile = jnp.where((y ^ offset) == i, share, tile)
        tiles.append(tile)
    total = jnp.concatenate(tiles, axis=0)
    width = total.shape[1]
    half, quarter, eighth = width // 2, width // 4, width // 8
    share = (eighth + eighth // 2) // 4
    packed = jnp.concatenate([total[i * 8 : i * 8 + share] for i in range(4)], axis=0)
    sums = total[share : share + 1]
    for i in range(1, 4):
        sums = sums + total[i * 8 + share : i * 8 + share + 1]
    upper, lower = packed[:eighth], packed[eighth:]
    parts = [upper, pltpu.roll(upper, half, 1)]
    for i in range(4):
        parts.append(pltpu.roll(lower, (quarter - i * quarter) % width, 1))
    wide = jnp.concatenate(parts + [jnp.zeros((half, width), f32)], axis=0)
    rows = lax.broadcasted_iota(jnp.int32, (half, width), 0)
    lanes = lax.broadcasted_iota(jnp.int32, (half, width), 1)
    gram = jnp.where(rows <= lanes, wide[:half], jnp.transpose(wide)[:half])

    def pair_rows(first, second):
        x, y = gram * first, gram * second
        return jnp.where(rows % 2 == 0, x + pltpu.roll(x, half - 1, 0), y + pltpu.roll(y, 1, 0))

    even = pair_rows(slope_ref[0], slope_ref[2])
    odd = pair_rows(slope_ref[1], slope_ref[3])
    newton = divisor * jnp.where(lanes % 2 == 0, even + pltpu.roll(even, width - 1, 1), odd + pltpu.roll(odd, 1, 1))
    newton_ref[...] = newton[:, :half]
    basis_slope = basis_slope_ref[...]
    lane = lanes[:1]
    same = jnp.sum(gram * basis_slope, axis=0, keepdims=True)
    turn = jnp.sum(swap_lanes(gram) * basis_slope, axis=0, keepdims=True)
    turn = jnp.where(lane % 2 == 0, turn, -turn)
    fitted = jnp.where(lane % 2 == 0, same + pltpu.roll(same, width - 1, 1), turn + pltpu.roll(turn, 1, 1))
    gradient_ref[...] = (-divisor * (sums - fitted))[:, :half]


def flips(n, bits):
    return [(i, i ^ bits) for i in range(n)]


def cost(flops, bytes_accessed):
    return pl.CostEstimate(flops=flops, bytes_accessed=bytes_accessed, transcendentals=0)


def local(frame_slab, pair_decay_rates, pair_angular_frequencies):
    points, epochs = frame_slab.shape
    pairs = pair_decay_rates.shape[0]
    basis = 2 * pairs
    width = 2 * basis
    tm_size, space_size = lax.axis_size("tm"), lax.axis_size("space")
    complete = epochs * tm_size
    half = points // 2
    quarter = half // 2
    divisor = 1.0 / (points * space_size * complete)
    in_hbm = lambda x: pltpu.with_memory_space_constraint(x, pltpu.HBM)
    rates = in_hbm(pair_decay_rates.reshape(1, pairs))
    freqs = in_hbm(pair_angular_frequencies.reshape(1, pairs))
    slab = in_hbm(frame_slab)
    scratch = [pltpu.VMEM((half, epochs), f32), pltpu.SemaphoreType.DMA((4,))]

    away, product_away, w, rates, freqs = pl.pallas_call(
        lambda *refs: first_kernel(complete, *refs),
        out_shape=(
            jax.ShapeDtypeStruct((quarter, width), f32),
            jax.ShapeDtypeStruct((quarter, width), f32),
            jax.ShapeDtypeStruct((epochs, 2 * width), bf16),
            jax.ShapeDtypeStruct((1, pairs), f32),
            jax.ShapeDtypeStruct((1, pairs), f32),
        ),
        in_specs=[HBM, HBM, HBM],
        out_specs=(VMEM,) * 5,
        scratch_shapes=scratch + [pltpu.SemaphoreType.DMA((2,))],
        compiler_params=PARAMS,
        name="project_away",
    )(slab, rates, freqs)
    arrived = lax.ppermute(away, "tm", flips(tm_size, 1))
    eighth = quarter // 2
    first, second, product = pl.pallas_call(
        second_kernel,
        out_shape=[jax.ShapeDtypeStruct((n, width), f32) for n in (eighth, eighth, quarter)],
        in_specs=[VMEM, VMEM],
        out_specs=[VMEM] * 3,
        compiler_params=PARAMS,
        cost_estimate=cost(2 * half * epochs * width * 4, half * epochs * 4),
        name="project_kept",
    )(frame_slab, w)

    near, wrap = flips(tm_size, 3), flips(tm_size, 7)
    first, second = first + arrived[:eighth], second + arrived[eighth:]
    product_away, first, second = lax.optimization_barrier((product_away, first, second))
    product_in = lax.ppermute(product_away, "tm", flips(tm_size, 1))
    first_in = lax.ppermute(first, "tm", near)
    second_in = lax.ppermute(second, "tm", wrap)
    gram, slopes, basis_slope = pl.pallas_call(
        lambda *refs: gram_kernel(complete, *refs),
        out_shape=(
            jax.ShapeDtypeStruct((basis, width), f32),
            jax.ShapeDtypeStruct((4, basis, width), f32),
            jax.ShapeDtypeStruct((basis, width), f32),
        ),
        in_specs=[VMEM, VMEM, ANY],
        out_specs=(VMEM, VMEM, VMEM),
        compiler_params=PARAMS,
        cost_estimate=cost(10**9, 10**7),
        name="grams",
    )(rates, freqs, product)
    first, gram = lax.optimization_barrier((first + first_in, gram))
    first_in = lax.ppermute(first, "tm", wrap)
    second, first = lax.optimization_barrier((second, first))
    second = second + second_in
    second_in = lax.ppermute(second, "tm", near)
    inverse_gram = pl.pallas_call(
        inverse_kernel,
        out_shape=jax.ShapeDtypeStruct((3 * width, 2 * width), bf16),
        in_specs=[VMEM, ANY],
        out_specs=VMEM,
        compiler_params=PARAMS,
        cost_estimate=cost(10**9, 10**7),
        name="inverse",
    )(gram, second)
    modes_half, message = pl.pallas_call(
        modes_kernel,
        out_shape=(
            jax.ShapeDtypeStruct((basis, half), f32),
            jax.ShapeDtypeStruct((8, width), f32),
        ),
        in_specs=[VMEM] * 7,
        out_specs=(VMEM, VMEM),
        compiler_params=PARAMS,
        name="modes",
    )(first, first_in, second, second_in, product, product_in, inverse_gram)

    message_in = lax.ppermute(message, "tm", flips(tm_size, 1))
    modes_other = lax.ppermute(modes_half, "tm", flips(tm_size, 1))
    messages = pl.pallas_call(
        spread_kernel,
        out_shape=jax.ShapeDtypeStruct((space_size, *message.shape), f32),
        in_specs=[VMEM, VMEM, ANY],
        out_specs=VMEM,
        compiler_params=PARAMS,
        name="spread",
    )(message, message_in, modes_other)
    messages = lax.all_to_all(messages, "space", 0, 0, axis_index_groups=[list(range(space_size))[::-1]])
    blocks = 8
    spatial_modes, misfit, done = pl.pallas_call(
        misfit_kernel,
        out_shape=(
            jax.ShapeDtypeStruct((basis, points), f32),
            jax.ShapeDtypeStruct((points, epochs), f32),
            jax.ShapeDtypeStruct((8, width), f32),
        ),
        in_specs=[HBM, VMEM, VMEM, VMEM],
        out_specs=(HBM, HBM, VMEM),
        scratch_shapes=[pltpu.VMEM((points, epochs), f32)] + [pltpu.SemaphoreType.DMA((n,)) for n in (blocks, blocks, 2)],
        compiler_params=PARAMS,
        cost_estimate=cost(10**9, 10**7),
        name="misfit",
    )(slab, modes_half, modes_other, w)
    total = pl.pallas_call(
        collect_kernel,
        out_shape=jax.ShapeDtypeStruct(message.shape, f32),
        in_specs=[VMEM, ANY],
        out_specs=VMEM,
        compiler_params=PARAMS,
        name="collect",
    )(messages, done)
    total_near = lax.ppermute(total, "tm", near)
    total_far = lax.ppermute(jnp.concatenate([total, total_near]), "tm", wrap)
    gradient, gauss_newton = pl.pallas_call(
        lambda *refs: last_kernel(divisor, *refs),
        out_shape=(
            jax.ShapeDtypeStruct((1, basis), f32),
            jax.ShapeDtypeStruct((basis, basis), f32),
        ),
        in_specs=[VMEM] * 5,
        out_specs=(VMEM, VMEM),
        compiler_params=PARAMS,
        name="newton",
    )(total, total_near, total_far, slopes, basis_slope)
    return spatial_modes, misfit, gradient.reshape(basis), gauss_newton


def solution(mesh):
    return jax.shard_map(
        local,
        mesh=mesh,
        in_specs=(P("space", "tm"), P(), P()),
        out_specs=(P(None, "space"), P("space", "tm"), P(), P()),
        check_vma=False,
    )
```
